32 devices in a mesh: row: 8 (over z, x), col: 4 (over y, core).
Axes of the slice: x: 2, y: 2, z: 4, core: 2. Of those that a mesh axis runs over, the one named last changes fastest.
Arguments:
- h_blocks: bfloat16 [4, 8, 16, 128, 128], P(None, 'row', 'col'), may hold values from -1.1953125 to 1.1953125
- p_blocks: bfloat16 [4, 8, 16, 128, 128], P(None, 'row', 'col'), may hold values from -1.1953125 to 1.1953125
- p1_blocks: bfloat16 [4, 8, 16, 128, 128], P(None, 'row', 'col'), may hold values from -1.1953125 to 1.1953125
- h_mask: int32 [4, 8, 16], P(None, 'row', 'col'), may hold values 0 or 1
- p_mask: int32 [4, 8, 16], P(None, 'row', 'col'), may hold values 0 or 1
- p1_mask: int32 [4, 8, 16], P(None, 'row', 'col'), may hold values 0 or 1
Outputs:
- commutator: bfloat16 [4, 8, 16, 128, 128], P(None, 'row', 'col')
- response: bfloat16 [4, 8, 16, 128, 128], P(None, 'row', 'col')
The draws below stay inside these ranges and needn't reach their ends.
All inputs are finite; a program needn't handle non-finite values. No bound on the sum of `h_mask` or of `p_mask` or of `p1_mask` on one device may be relied on, other than what follows from the above.
Results may differ from the reference program's by a relative error of at most 0.001.
Values may be sent and summed in bfloat16 or wider, within the bound.
No kernel may reach another device: no remote copies, remote signals or barrier semaphores. Data moves between devices by JAX's collectives and lax.ppermute only.
A program may use at most 128 MiB of HBM per device.

```python
import jax
import jax.numpy as jnp

B = 128
K = 16
ROWS_DEV = 4
ROW_OWNERS = 8
BLOCK_ROWS = 32
N_ROW = 8
N_COL = 4


def place_ends(entries, stream_key, low, largest):
    dims = entries.shape
    spot = [jax.random.randint(jax.random.fold_in(stream_key, axis), (), 0, dims[axis]) for axis in range(len(dims))]
    entries = entries.at[tuple(spot)].set(low)
    longest = dims.index(max(dims))
    spot[longest] = (spot[longest] + 1) % dims[longest]
    return entries.at[tuple(spot)].set(largest)


def block_levels(stream_key, extent, cuts, low, high):
    def one(axis_at, parts):
        heights = jax.random.uniform(jax.random.fold_in(jax.random.fold_in(stream_key, 6), axis_at), (parts,), jnp.float32, low / len(cuts), high / len(cuts))
        return jnp.repeat(jnp.exp(heights), extent[axis_at] // parts).reshape((-1,) + (1,) * (len(extent) - axis_at - 1))

    factor_of = one(*cuts[0])
    for cut in cuts[1:]:
        factor_of = factor_of * one(*cut)
    return factor_of


def normal_values(rng, extent, scale, bound, pieces=(), kind=jnp.bfloat16):
    result = scale * jax.random.normal(rng, extent, jnp.float32)
    if pieces:
        result = result * block_levels(rng, extent, pieces, -0.22, 0.18)
    return jnp.clip(result, -bound, bound).astype(kind)


def setup_inputs(seed: int = 0) -> dict:
    keys = jax.random.split(jax.random.key(seed), 7)
    return {
        "h_blocks": normal_values(keys[0], (ROWS_DEV, ROW_OWNERS, K, B, B), 0.2, 1.1953125, ((1, 8), (2, 4))),
        "p_blocks": normal_values(keys[1], (ROWS_DEV, ROW_OWNERS, K, B, B), 0.2, 1.1953125, ((1, 8), (2, 4))),
        "p1_blocks": normal_values(keys[2], (ROWS_DEV, ROW_OWNERS, K, B, B), 0.2, 1.1953125, ((1, 8), (2, 4))),
        "h_mask": place_ends((jax.random.randint(keys[3], (ROWS_DEV, ROW_OWNERS, K), 0, 4) < 3).astype(jnp.int32), jax.random.fold_in(keys[3], 1), 0, 1),
        "p_mask": place_ends((jax.random.randint(keys[4], (ROWS_DEV, ROW_OWNERS, K), 0, 4) < 3).astype(jnp.int32), jax.random.fold_in(keys[4], 1), 0, 1),
        "p1_mask": place_ends((jax.random.randint(keys[5], (ROWS_DEV, ROW_OWNERS, K), 0, 4) < 3).astype(jnp.int32), jax.random.fold_in(keys[5], 1), 0, 1),
    }


def band_layout():
    half_band = K // 2
    slot_count = K // N_COL
    local_row = jnp.arange(ROWS_DEV, dtype=jnp.int32)[:, None, None]
    owner_row = jnp.arange(N_ROW, dtype=jnp.int32)[None, :, None]
    slot_index = jnp.arange(K, dtype=jnp.int32)[None, None, :]
    block_row = owner_row + N_ROW * local_row + 0 * slot_index
    owner_col = slot_index // slot_count
    position = (owner_col - block_row + half_band) % N_COL + N_COL * (slot_index % slot_count)
    return block_row.astype(jnp.int32), position.astype(jnp.int32)


def to_band(values, pattern, block_row, position):
    kept_values = values * pattern[..., None, None].astype(values.dtype)
    return jnp.zeros((BLOCK_ROWS, K, B, B), values.dtype).at[block_row, position].set(kept_values)


def product(left_band, right_band):
    half_band = K // 2
    summed = jnp.zeros((BLOCK_ROWS, K, B, B), jnp.float32)
    for offset in range(-half_band, half_band):
        shifted = jnp.roll(right_band, -offset, axis=0)
        first_out = max(-half_band, offset - half_band)
        last_out = min(half_band - 1, offset + half_band - 1)
        left_column = left_band[:, offset + half_band].astype(jnp.float32)
        right_part = shifted[:, first_out - offset + half_band:last_out - offset + half_band + 1].astype(jnp.float32)
        partial_sum = jnp.einsum('qij,qtjl->qtil', left_column, right_part)
        summed = summed.at[:, first_out + half_band:last_out + half_band + 1].add(partial_sum)
    return summed


def reference(h_blocks, p_blocks, p1_blocks, h_mask, p_mask, p1_mask):
    block_row, position = band_layout()
    h_band = to_band(h_blocks, h_mask, block_row, position)
    p_band = to_band(p_blocks, p_mask, block_row, position)
    p1_band = to_band(p1_blocks, p1_mask, block_row, position)
    output_pattern = p1_mask[..., None, None].astype(jnp.float32)
    commuted = product(h_band, p1_band) - product(p1_band, h_band)
    purified = product(p_band, p1_band) + product(p1_band, p_band)
    commutator = (commuted[block_row, position] * output_pattern).astype(jnp.bfloat16)
    response = (purified[block_row, position] * output_pattern).astype(jnp.bfloat16)
    return commutator, response
```

```python
import functools

import jax
import jax.numpy as jnp
import numpy as np
from jax import lax
from jax.experimental import pallas as pl
from jax.experimental.pallas import tpu as pltpu
from jax.sharding import PartitionSpec as P

H, Q, D = 0, 1, 2
AXES = ("row", "col")


class Plan:
    def __init__(self, row_count, col_count, rows_dev, slot_count):
        self.R, self.C, self.M, self.S = row_count, col_count, rows_dev, slot_count
        self.Z, self.Y = row_count // 2, col_count // 2
        self.K = slot_count * col_count
        self.half = self.K // 2
        reach = (self.half + 1) // 2
        self.ring = 2 * reach + 1 <= self.Z
        self.steps = reach if self.ring else self.Z - 1
        self.nb = -(-self.K // self.R)
        self.units = [(0, 0)]
        for step in range(1, self.steps + 1):
            self.units += [(-1, step), (1, step)]

    def pairs(self, target):
        found = []
        for z in range(self.Z):
            for x in range(2):
                for y in range(self.Y):
                    for k in range(2):
                        to = target(z, x, y, k)
                        if to is not None:
                            tz, tx, ty, tk = to
                            found.append(
                                ((2 * z + x) * self.C + 2 * y + k, (2 * tz + tx) * self.C + 2 * ty + tk)
                            )
        return found

    def holds(self, z, way, step):
        return self.ring or 0 <= z + way * step < self.Z

    def flow(self, way, step):
        def target(z, x, y, k):
            to = z - way
            if not self.ring and not (0 <= to < self.Z and self.holds(to, way, step)):
                return None
            return to % self.Z, x, y, k

        return self.pairs(target)

    def table(self):
        R, C, S, M, Y = self.R, self.C, self.S, self.M, self.Y
        out = np.zeros((R, C, len(self.units), 2 + 2 * self.nb * 4), np.int32)
        for r in range(R):
            for c in range(C):
                z, x, y, k = r // 2, r % 2, c // 2, c % 2
                for u, (way, step) in enumerate(self.units):
                    delta = way * step
                    out[r, c, u, 0] = self.holds(z, way, step)
                    out[r, c, u, 1] = ((z + delta) % self.Z % Y - y) % Y
                    for e in range(2):
                        rho = k ^ e
                        base = 2 * delta + k - rho
                        phase = (2 * y + x - 2 * z - rho + self.half) % C
                        first = -((self.half + base) // R)
                        for n in range(self.nb):
                            w = first + n
                            b = base + R * w
                            ok = -self.half <= b < self.half
                            at = 2 + (e * self.nb + n) * 4
                            out[r, c, u, at:at + 4] = (
                                ((b + self.half) // C if ok else 0),
                                w % M,
                                (phase - b) // C,
                                ok,
                            )
        return out


def contract_body(plan, wanted, has_start, tab, a_ref, *refs):
    count = len(wanted)
    unit_refs = refs[:2 * count]
    refs = refs[2 * count:]
    start_ref = None
    if has_start:
        start_ref, refs = refs[0], refs[1:]
    total_ref, held, sem = refs
    e, m = pl.program_id(0), pl.program_id(1)
    first = jnp.logical_and(e == 0, m == 0)
    S, M, nb = plan.S, plan.M, plan.nb
    B = held.shape[-1]

    def copies(u):
        return (
            pltpu.make_async_copy(unit_refs[2 * u], held.at[u, pl.ds(0, 2)], sem.at[u, 0]),
            pltpu.make_async_copy(unit_refs[2 * u + 1], held.at[u, D], sem.at[u, 1]),
        )

    for u, unit in enumerate(wanted):
        @pl.when(jnp.logical_and(first, tab[unit, 0] == 1))
        def _(u=u):
            for copy in copies(u):
                copy.start()

    if has_start:
        total_ref[...] = start_ref[...]
    else:
        total_ref[...] = jnp.zeros_like(total_ref)

    for u, unit in enumerate(wanted):
        @pl.when(tab[unit, 0] == 1)
        def _(u=u, unit=unit):
            @pl.when(first)
            def _():
                for copy in copies(u):
                    copy.wait()

            dy = tab[unit, 1]
            terms = []
            for n in range(nb):
                at = 2 + (e * nb + n) * 4
                terms.append(tuple(tab[unit, at + i] for i in range(4)))

            def left(mat):
                return jnp.concatenate([a_ref[0, dy, mat, 0, slot] for slot, _, _, _ in terms], axis=1)

            def right(mat):
                rows = []
                for _, row_shift, slot_shift, ok in terms:
                    row = lax.rem(m + row_shift, M)
                    cols = []
                    for s in range(S):
                        slot = s + slot_shift
                        inside = jnp.logical_and(ok == 1, jnp.logical_and(slot >= 0, slot < S))
                        block = held[u, mat, row, jnp.clip(slot, 0, S - 1)]
                        cols.append(jnp.where(inside, block, jnp.zeros_like(block)))
                    rows.append(jnp.concatenate(cols, axis=1))
                return jnp.concatenate(rows, axis=0)

            dot = functools.partial(jnp.dot, preferred_element_type=jnp.float32)
            both = dot(jnp.concatenate([left(H), left(D)], axis=0), right(Q))
            mine = left(Q)
            commutator = both[:B] - dot(mine, right(H))
            response = both[B:] + dot(mine, right(D))
            for s in range(S):
                total_ref[0, 0, 0, s] += commutator[:, s * B:(s + 1) * B]
                total_ref[0, 1, 0, s] += response[:, s * B:(s + 1) * B]


def contract(plan, tab, a_units, wanted, unit_arrays, start):
    M, S, Y = plan.M, plan.S, plan.Y
    B = a_units.shape[-1]
    total_block = pl.BlockSpec((1, 2, 1, S, B, B), lambda e, m, tab: (e, 0, m, 0, 0, 0))
    operands = [a_units]
    specs = [pl.BlockSpec((1, Y, 3, 1, S, B, B), lambda e, m, tab: (e, 0, 0, m, 0, 0, 0))]
    for arrays in unit_arrays:
        operands += list(arrays)
        specs += [pl.BlockSpec(memory_space=pl.ANY)] * 2
    if start is not None:
        operands.append(start)
        specs.append(total_block)
    terms = 2 * M * len(wanted) * plan.nb * S * 4
    return pl.pallas_call(
        functools.partial(contract_body, plan, tuple(wanted), start is not None),
        grid_spec=pltpu.PrefetchScalarGridSpec(
            num_scalar_prefetch=1,
            grid=(2, M),
            in_specs=specs,
            out_specs=total_block,
            scratch_shapes=[
                pltpu.VMEM((len(wanted), 3, M, S, B, B), a_units.dtype),
                pltpu.SemaphoreType.DMA((len(wanted), 2)),
            ],
        ),
        out_shape=jax.ShapeDtypeStruct((2, 2, M, S, B, B), jnp.float32),
        compiler_params=pltpu.CompilerParams(vmem_limit_bytes=32 * 2**20),
        cost_estimate=pl.CostEstimate(
            flops=2 * B**3 * terms,
            bytes_accessed=a_units.size * 2 + len(wanted) * 3 * M * S * B * B * 2,
            transcendentals=0,
        ),
    )(tab, *operands)


def per_device(plan, h_blocks, p_blocks, p1_blocks, h_mask, p_mask, p1_mask):
    def kept(values, pattern):
        return values[:, 0] * pattern[:, 0][:, :, None, None].astype(values.dtype)

    def move(value, pairs):
        return lax.ppermute(value, AXES, pairs)

    row, col = lax.axis_index("row"), lax.axis_index("col")
    tab = jnp.asarray(plan.table())[row, col]
    swapped = (row % 2) != (col % 2)

    own_hq = jnp.stack([kept(h_blocks, h_mask), kept(p1_blocks, p1_mask)])
    own_d = kept(p_blocks, p_mask)

    cross = plan.pairs(lambda z, x, y, k: (z, k, y, x))
    sibling = plan.pairs(lambda z, x, y, k: (z, x, y, 1 - k))
    x_swap = plan.pairs(lambda z, x, y, k: (z, 1 - x, y, k))

    got = {(0, 0): (move(own_hq, cross), move(own_d, cross))}
    for step in range(1, plan.steps + 1):
        for way in (-1, 1):
            before = got[(way, step - 1) if step > 1 else (0, 0)]
            pairs = plan.flow(way, step)
            got[(way, step)] = tuple(move(part, pairs) for part in before)

    own = jnp.concatenate([own_hq, own_d[None]])
    across = move(own, x_swap)
    by_x = ([own], [across])
    for dy in range(1, plan.Y):
        pairs = plan.pairs(lambda z, x, y, k: (z, x, (y - dy) % plan.Y, k))
        by_x[0].append(move(own, pairs))
        by_x[1].append(move(across, pairs))
    near, far = jnp.stack(by_x[0]), jnp.stack(by_x[1])
    a_units = jnp.stack([jnp.where(swapped, far, near), jnp.where(swapped, near, far)])

    every = list(range(len(plan.units)))
    early, late = every[:-2], every[-2:]
    total = contract(plan, tab, a_units, early, [got[plan.units[u]] for u in early], None)
    total = contract(plan, tab, a_units, late, [got[plan.units[u]] for u in late], total)

    result = (total[0] + move(total[1], sibling)).astype(jnp.bfloat16)
    result = move(result, cross)
    pattern = p1_mask[:, 0][None, :, :, None, None].astype(result.dtype)
    result = result * pattern
    return result[0][:, None], result[1][:, None]


def solution(mesh):
    blocks = P(None, "row", "col", None, None)
    masks = P(None, "row", "col")

    def run(h_blocks, p_blocks, p1_blocks, h_mask, p_mask, p1_mask):
        plan = Plan(
            mesh.shape["row"], mesh.shape["col"], h_blocks.shape[0], h_blocks.shape[2] // mesh.shape["col"]
        )
        return jax.shard_map(
            functools.partial(per_device, plan),
            mesh=mesh,
            in_specs=(blocks,) * 3 + (masks,) * 3,
            out_specs=(blocks,) * 2,
            check_vma=False,
        )(h_blocks, p_blocks, p1_blocks, h_mask, p_mask, p1_mask)

    return run
```

```python
import functools
import itertools

import jax
import jax.numpy as jnp
import numpy as np
from jax import lax
from jax.experimental import pallas as pl
from jax.experimental.pallas import tpu as pltpu
from jax.sharding import PartitionSpec as P

H, Q, D = 0, 1, 2
AXES = ("row", "col")


class Plan:
    def __init__(self, row_count, col_count, rows_dev, slot_count):
        self.R, self.C, self.M, self.S = row_count, col_count, rows_dev, slot_count
        self.Z, self.Y = row_count // 2, col_count // 2
        self.K = slot_count * col_count
        self.half = self.K // 2
        self.nb = -(-self.K // self.R)
        reach = (self.half + 1) // 2
        Z = self.Z
        ring = 2 * reach + 1 <= Z
        self.quad = Z == 4 and not ring
        if self.quad:
            inward, middle, outward = [(0, 1), (3, 2)], [(1, 2), (2, 1)], [(1, 0), (2, 3)]
            self.hops = [
                ("mid", "own", middle), ("out1", "own", outward), ("in", "own", inward),
                ("mid2", "in", middle), ("out2", "mid", outward), ("out3", "mid2", outward),
            ]
        else:
            self.hops = []
            for step in range(1, (reach if ring else Z - 1) + 1):
                for name, way in (("up", 1), ("down", -1)):
                    ends = [(z, z + way) for z in range(Z)]
                    ends = [(z, to % Z) for z, to in ends if ring or 0 <= to < Z and 0 <= z - way * (step - 1) < Z]
                    self.hops.append((name + str(step), name + str(step - 1) if step > 1 else "own", ends))
        self.origin = {"own": {z: z for z in range(Z)}}
        for name, source, ends in self.hops:
            self.origin[name] = {to: self.origin[source][z] for z, to in ends}
        self.units = list(self.origin)

    def pairs(self, target, planes=None):
        found = []
        for z in range(self.Z) if planes is None else planes:
            for x in range(2):
                for y in range(self.Y):
                    for k in range(2):
                        to = target(z, x, y, k)
                        if to is not None:
                            tz, tx, ty, tk = to
                            found.append(
                                ((2 * z + x) * self.C + 2 * y + k, (2 * tz + tx) * self.C + 2 * ty + tk)
                            )
        return found

    def along_z(self, ends):
        ends = dict(ends)
        return self.pairs(lambda z, x, y, k: (ends[z], x, y, k) if z in ends else None)

    def table(self):
        R, C, M, Y = self.R, self.C, self.M, self.Y
        out = np.zeros((R, C, len(self.units) + 1, 2 + 2 * self.nb * 4), np.int32)
        for r in range(R):
            for c in range(C):
                z, x, y, k = r // 2, r % 2, c // 2, c % 2
                out[r, c, -1, 0] = x != k
                for u, unit in enumerate(self.units):
                    if z not in self.origin[unit]:
                        continue
                    there = self.origin[unit][z]
                    out[r, c, u, 0] = 1
                    out[r, c, u, 1] = (there % Y - y) % Y
                    for e in range(2):
                        rho = k ^ e
                        base = 2 * (there - z) + k - rho
                        phase = (2 * y + x - 2 * z - rho + self.half) % C
                        first = -((self.half + base) // R)
                        for n in range(self.nb):
                            w = first + n
                            b = base + R * w
                            ok = -self.half <= b < self.half
                            at = 2 + (e * self.nb + n) * 4
                            out[r, c, u, at:at + 4] = (
                                ((b + self.half) // C if ok else 0),
                                w % M,
                                (phase - b) // C,
                                ok,
                            )
        return out


def right_side(plan, terms, m, block_at):
    S, M = plan.S, plan.M
    parts = []
    for n, (_, row_shift, slot_shift, ok) in enumerate(terms):
        row = lax.rem(m + row_shift, M)
        cols = []
        for s in range(S):
            slot = s + slot_shift
            inside = jnp.logical_and(ok == 1, jnp.logical_and(slot >= 0, slot < S))
            block = block_at(n, row, jnp.clip(slot, 0, S - 1))
            cols.append(jnp.where(inside, block, jnp.zeros_like(block)))
        parts.append(jnp.concatenate(cols, axis=1))
    return jnp.concatenate(parts, axis=0)


def terms_of(plan, tab, unit, e):
    at = 2 + e * plan.nb * 4
    return [tuple(tab[unit, at + 4 * n + i] for i in range(4)) for n in range(plan.nb)]


def contract_body(plan, wanted, kinds, spans, tab, *refs):
    low, high = (0 if H in kinds else 1), (3 if D in kinds else 2)
    data, refs = refs[:len(spans)], refs[len(spans):]
    total_refs, (held, rows, sem, row_sem) = refs[:2], refs[2:]
    S, M, Y = plan.S, plan.M, plan.Y
    B = held.shape[-1]
    swapped = tab[len(plan.units), 0]
    valid = [tab[unit, 0] == 1 for unit in wanted]
    some = functools.reduce(jnp.logical_or, valid)

    def copies(use, into, into_sem):
        for i, (what, a, b) in enumerate(spans):
            a, b, first = max(a, low), min(b, high), a
            if what == use and a < b:
                yield pltpu.make_async_copy(
                    data[i].at[pl.ds(a - first, b - a)], into.at[pl.ds(a - low, b - a)], into_sem.at[a - low]
                )

    def unit_copies(u):
        return copies(("unit", u), held.at[u], sem.at[u])

    for flip in range(2):
        @pl.when(jnp.logical_and(some, swapped == flip))
        def _(flip=flip):
            for side, dy in itertools.product(range(2), range(Y)):
                into = (side ^ flip, dy)
                for copy in copies(("rows", side, dy), rows.at[into], row_sem.at[into]):
                    copy.start()
    for u in range(len(wanted)):
        @pl.when(valid[u])
        def _(u=u):
            for copy in unit_copies(u):
                copy.start()

    for total_ref in total_refs:
        total_ref[...] = jnp.zeros_like(total_ref)

    for flip in range(2):
        @pl.when(jnp.logical_and(some, swapped == flip))
        def _(flip=flip):
            for side, dy in itertools.product(range(2), range(Y)):
                into = (side ^ flip, dy)
                for copy in copies(("rows", side, dy), rows.at[into], row_sem.at[into]):
                    copy.wait()

    for u, unit in enumerate(wanted):
        @pl.when(valid[u])
        def _(u=u, unit=unit):
            for copy in unit_copies(u):
                copy.wait()
            dy = tab[unit, 1]
            for e in range(2):
                terms = terms_of(plan, tab, unit, e)

                @pl.loop(0, M, unroll=True)
                def _(m, e=e, terms=terms):
                    def left(mat):
                        return jnp.concatenate([rows[e, dy, mat - low, m, slot] for slot, _, _, _ in terms], axis=1)

                    def right(mat):
                        return right_side(plan, terms, m, lambda n, row, slot: held[u, mat - low, row, slot])

                    dot = functools.partial(jnp.dot, preferred_element_type=jnp.float32)
                    both = dot(jnp.concatenate([left(kind) for kind in kinds], axis=0), right(Q))
                    mine = left(Q)
                    for i, kind in enumerate(kinds):
                        there, back = both[i * B:(i + 1) * B], dot(mine, right(kind))
                        sums = there - back if kind == H else there + back
                        for s in range(S):
                            total_refs[e][i, m, s] += sums[:, s * B:(s + 1) * B]


def contract(plan, tab, near, far, wanted, kinds, got):
    M, S, Y = plan.M, plan.S, plan.Y
    operands, spans = [], []
    for u, unit in enumerate(wanted):
        for array, first in got[unit]:
            operands.append(array)
            spans.append((("unit", u), first, first + array.shape[0]))
    for side, lists in enumerate((near, far)):
        for dy, pieces in enumerate(lists):
            for array, first in pieces:
                operands.append(array)
                spans.append((("rows", side, dy), first, first + array.shape[0]))
    B, kind_of = operands[0].shape[-1], operands[0].dtype
    mats = 1 + len(kinds)
    specs = [pl.BlockSpec(memory_space=pl.ANY)] * len(operands)
    whole = pl.BlockSpec(memory_space=pltpu.VMEM)
    terms = 2 * M * min(len(wanted), plan.Z) * plan.nb * S * 2 * len(kinds)
    return pl.pallas_call(
        functools.partial(
            contract_body, plan, tuple(plan.units.index(unit) for unit in wanted), kinds, tuple(spans)
        ),
        in_specs=[pl.BlockSpec(memory_space=pltpu.SMEM)] + specs,
        out_specs=[whole] * 2,
        scratch_shapes=[
            pltpu.VMEM((len(wanted), mats, M, S, B, B), kind_of),
            pltpu.VMEM((2, Y, mats, M, S, B, B), kind_of),
            pltpu.SemaphoreType.DMA((len(wanted), mats)),
            pltpu.SemaphoreType.DMA((2, Y, mats)),
        ],
        out_shape=[jax.ShapeDtypeStruct((len(kinds), M, S, B, B), jnp.float32)] * 2,
        compiler_params=pltpu.CompilerParams(vmem_limit_bytes=58 * 2**20),
        cost_estimate=pl.CostEstimate(
            flops=6 * B**3 * terms,
            bytes_accessed=len(spans) * M * S * B * B * 2,
            transcendentals=0,
        ),
    )(tab, *operands)


def find(pieces, mat):
    for ref, first in pieces:
        if first <= mat < first + ref.shape[0]:
            return ref, mat - first


def last_body(plan, kind, firsts, tab, kept, given, *refs):
    data, (kept_out, given_out, rows, held, sem) = refs[:-5], refs[-5:]
    S, M, Y, nb = plan.S, plan.M, plan.Y, plan.nb
    B = held.shape[-1]
    unit = len(plan.units) - 1
    valid = tab[unit, 0] == 1
    swapped = tab[unit + 1, 0]
    terms = [terms_of(plan, tab, unit, e) for e in range(2)]
    totals = kept_out, given_out
    places = {}
    for at, (name, first) in enumerate(firsts):
        places.setdefault(name, []).append((data[at], first))

    def base_copies():
        for i, ref in enumerate((kept, given)):
            yield pltpu.make_async_copy(ref.at[kind // 2], totals[i], sem.at[0, i, 0])

    def unit_copies():
        for i, mat in enumerate((kind, Q)):
            ref, index = find(places["unit"], mat)
            yield pltpu.make_async_copy(ref.at[index], held.at[i], sem.at[0, i, 1])

    def row_copies(e, pieces):
        for i, mat in enumerate((kind, Q)):
            ref, index = find(pieces, mat)
            for n in range(nb):
                yield pltpu.make_async_copy(ref.at[index, :, terms[e][n][0]], rows.at[e, i, n], sem.at[1 + e, i, n])

    def fetch(verb):
        @pl.when(valid)
        def _():
            for copy in unit_copies():
                verb(copy)

        for flip, dy in itertools.product(range(2), range(Y)):
            @pl.when(jnp.logical_and(valid, jnp.logical_and(swapped == flip, tab[unit, 1] == dy)))
            def _(flip=flip, dy=dy):
                for side in range(2):
                    for copy in row_copies(side ^ flip, places["rows", side, dy]):
                        verb(copy)

        for copy in base_copies():
            verb(copy)

    fetch(lambda copy: copy.start())
    fetch(lambda copy: copy.wait())

    @pl.when(valid)
    def _():
        for e in (1, 0):
            @pl.loop(0, M, unroll=True)
            def _(m, e=e):
                def left(i):
                    return jnp.concatenate([rows[e, i, n, m] for n in range(nb)], axis=1)

                def right(i):
                    return right_side(plan, terms[e], m, lambda n, row, slot: held[i, row, slot])

                dot = functools.partial(jnp.dot, preferred_element_type=jnp.float32)
                there, back = dot(left(0), right(1)), dot(left(1), right(0))
                more = there - back if kind == H else there + back
                for s in range(S):
                    totals[e][m, s] += more[:, s * B:(s + 1) * B]


def last(plan, tab, kind, kept, given, near, far, unit):
    M, S, Y, nb = plan.M, plan.S, plan.Y, plan.nb
    lists = [("unit", unit)]
    lists += [(("rows", side, dy), pieces) for side, sides in enumerate((near, far)) for dy, pieces in enumerate(sides)]
    firsts = tuple((name, first) for name, pieces in lists for _, first in pieces)
    operands = [array for _, pieces in lists for array, _ in pieces]
    B = kept.shape[-1]
    return pl.pallas_call(
        functools.partial(last_body, plan, kind, firsts),
        in_specs=[pl.BlockSpec(memory_space=pltpu.SMEM)] + [pl.BlockSpec(memory_space=pl.ANY)] * (2 + len(operands)),
        out_specs=[pl.BlockSpec(memory_space=pltpu.VMEM)] * 2,
        scratch_shapes=[
            pltpu.VMEM((2, 2, nb, M, B, B), operands[0].dtype),
            pltpu.VMEM((2, M, S, B, B), operands[0].dtype),
            pltpu.SemaphoreType.DMA((3, 2, max(nb, 2))),
        ],
        out_shape=[jax.ShapeDtypeStruct((M, S, B, B), jnp.float32)] * 2,
        compiler_params=pltpu.CompilerParams(vmem_limit_bytes=58 * 2**20),
        cost_estimate=pl.CostEstimate(flops=4 * 10**10, bytes_accessed=8 * 2**20, transcendentals=0),
    )(tab, kept, given, *operands)


def keep_body(*refs):
    count = len(refs) // 2
    masks, values, out = refs[:count], refs[count:-1], refs[-1]
    m = pl.program_id(0)
    for i, value in enumerate(values):
        for s in range(value.shape[2]):
            block = value[0, 0, s]
            out[i, 0, s] = jnp.where(masks[i][m, 0, s] != 0, block, jnp.zeros_like(block))


def keep(values, masks):
    M, _, S, B, _ = values[0].shape
    return pl.pallas_call(
        keep_body,
        grid=(M,),
        in_specs=[pl.BlockSpec(memory_space=pltpu.SMEM)] * len(masks)
        + [pl.BlockSpec((1, 1, S, B, B), lambda m: (m, 0, 0, 0, 0))] * len(values),
        out_specs=pl.BlockSpec((len(values), 1, S, B, B), lambda m: (0, m, 0, 0, 0)),
        out_shape=jax.ShapeDtypeStruct((len(values), M, S, B, B), values[0].dtype),
    )(*masks, *values)


def tick_body(token, out):
    out[...] = token[...]


def tick(token, *done, cost=2 * 10**10):
    token = lax.optimization_barrier((token, *done))[0]
    return pl.pallas_call(
        tick_body,
        out_shape=jax.ShapeDtypeStruct(token.shape, token.dtype),
        cost_estimate=pl.CostEstimate(flops=cost, bytes_accessed=0, transcendentals=0),
    )(token)


def move(value, pairs):
    return lax.ppermute(value, AXES, pairs)


def after(value, *others):
    return lax.optimization_barrier((value, *others))[0]


def per_device(plan, h_blocks, p_blocks, p1_blocks, h_mask, p_mask, p1_mask):
    row, col = lax.axis_index("row"), lax.axis_index("col")
    tab = jnp.asarray(plan.table())[row, col]
    mine = keep((h_blocks, p1_blocks, p_blocks), (h_mask, p1_mask, p_mask))
    pattern = p1_mask[:, 0][:, :, None, None].astype(jnp.bfloat16)

    cross = plan.pairs(lambda z, x, y, k: (z, k, y, x))
    sibling = plan.pairs(lambda z, x, y, k: (z, x, y, 1 - k))
    x_swap = plan.pairs(lambda z, x, y, k: (z, 1 - x, y, k))
    x_pairs = plan.pairs(lambda z, x, y, k: (z, 1 - x, y, k) if x == k else (z, x, y, 1 - k))
    y_pairs = [plan.pairs(lambda z, x, y, k: (z, x, (y - dy) % plan.Y, k)) for dy in range(1, plan.Y)]

    unit = move(mine, cross)
    hops = {name: (source, plan.along_z(ends)) for name, source, ends in plan.hops}
    if not plan.quad:
        got = {"own": unit}
        for name, (source, pairs) in hops.items():
            got[name] = move(got[source], pairs)
        across = move(unit, x_pairs)
        near = [[(mine, 0)]] + [[(move(mine, pairs), 0)] for pairs in y_pairs]
        far = [[(across, 0)]] + [[(move(across, pairs), 0)] for pairs in y_pairs]
        got = {name: [(value, 0)] for name, value in got.items()}
        kept, given = contract(plan, tab, near, far, plan.units, (H, D), got)
        results = move((kept + move(given, sibling)).astype(jnp.bfloat16), cross)
        return tuple((result * pattern)[:, None] for result in results)

    token = jnp.zeros((8, 128), jnp.float32)
    flight = [unit]
    got = {"own": {Q: unit[1:], H: unit[:1]}}

    def along(names, part):
        for name in names:
            source, pairs = hops[name]
            got.setdefault(name, {})[part] = sent(got[source][part], pairs)

    def sent(value, pairs):
        result = move(after(value, token), pairs)
        group.append(result)
        return result

    def closed():
        return tick(token, *flight), group, []

    group = []
    along(("mid", "out1", "in"), Q)
    token, flight, group = closed()
    along(("mid", "out1", "in"), H)
    beside = [sent(mine, pairs) for pairs in y_pairs]
    across = sent(unit, x_pairs)
    token, flight, group = closed()
    along(("mid2", "out2"), Q)
    token, flight, group = closed()
    along(("mid2", "out2"), H)
    far_qd = [sent(across[1:], pairs) for pairs in y_pairs]
    far_h = [sent(value[:1], x_swap) for value in beside]
    token, flight, group = closed()
    along(("out3",), Q)
    token, flight, group = closed()
    along(("out3",), H)

    near = [[(mine, H)]] + [[(value, H)] for value in beside]
    far = [[(across, H)]] + [[(a, H), (b, Q)] for a, b in zip(far_h, far_qd)]
    early = ["own", "in", "mid", "out1", "mid2", "out2"]
    pieces = {name: [(parts[H], H), (parts[Q], Q)] for name, parts in got.items()}
    kept, given = contract(plan, after(tab, token), near, far, early, (H, D), pieces)
    own, lent = last(plan, tab, D, kept, given, near, far, pieces["out3"][1:])
    response = own, move(lent, sibling)
    own, lent = last(plan, after(tab, own), H, kept, given, near, far, pieces["out3"])
    commutator = own, move(lent, sibling)
    results = [move((own + lent).astype(jnp.bfloat16), cross) for own, lent in (response, commutator)]
    response, commutator = [(result * pattern)[:, None] for result in results]
    return commutator, response


def solution(mesh):
    blocks = P(None, "row", "col", None, None)
    masks = P(None, "row", "col")

    def run(h_blocks, p_blocks, p1_blocks, h_mask, p_mask, p1_mask):
        plan = Plan(
            mesh.shape["row"], mesh.shape["col"], h_blocks.shape[0], h_blocks.shape[2] // mesh.shape["col"]
        )
        return jax.shard_map(
            functools.partial(per_device, plan),
            mesh=mesh,
            in_specs=(blocks,) * 3 + (masks,) * 3,
            out_specs=(blocks,) * 2,
            check_vma=False,
        )(h_blocks, p_blocks, p1_blocks, h_mask, p_mask, p1_mask)

    return run
```

```python
import functools
import itertools

import jax
import jax.numpy as jnp
import numpy as np
from jax import lax
from jax.experimental import pallas as pl
from jax.experimental.pallas import tpu as pltpu
from jax.sharding import PartitionSpec as P

H, Q, D = 0, 1, 2
AXES = ("row", "col")


class Plan:
    def __init__(self, row_count, col_count, rows_dev, slot_count):
        self.R, self.C, self.M, self.S = row_count, col_count, rows_dev, slot_count
        self.Z, self.Y = row_count // 2, col_count // 2
        self.K = slot_count * col_count
        self.half = self.K // 2
        self.nb = -(-self.K // self.R)
        reach = (self.half + 1) // 2
        Z = self.Z
        ring = 2 * reach + 1 <= Z
        self.quad = Z == 4 and not ring
        if self.quad:
            inward, middle, outward = [(0, 1), (3, 2)], [(1, 2), (2, 1)], [(1, 0), (2, 3)]
            self.hops = [
                ("mid", "own", middle), ("out1", "own", outward), ("in", "own", inward),
                ("mid2", "in", middle), ("out2", "mid", outward), ("out3", "mid2", outward),
            ]
        else:
            self.hops = []
            for step in range(1, (reach if ring else Z - 1) + 1):
                for name, way in (("up", 1), ("down", -1)):
                    ends = [(z, z + way) for z in range(Z)]
                    ends = [(z, to % Z) for z, to in ends if ring or 0 <= to < Z and 0 <= z - way * (step - 1) < Z]
                    self.hops.append((name + str(step), name + str(step - 1) if step > 1 else "own", ends))
        self.origin = {"own": {z: z for z in range(Z)}}
        for name, source, ends in self.hops:
            self.origin[name] = {to: self.origin[source][z] for z, to in ends}
        self.units = list(self.origin)

    def pairs(self, target, planes=None):
        found = []
        for z in range(self.Z) if planes is None else planes:
            for x in range(2):
                for y in range(self.Y):
                    for k in range(2):
                        to = target(z, x, y, k)
                        if to is not None:
                            tz, tx, ty, tk = to
                            found.append(
                                ((2 * z + x) * self.C + 2 * y + k, (2 * tz + tx) * self.C + 2 * ty + tk)
                            )
        return found

    def along_z(self, ends):
        ends = dict(ends)
        return self.pairs(lambda z, x, y, k: (ends[z], x, y, k) if z in ends else None)

    def table(self):
        R, C, M, Y = self.R, self.C, self.M, self.Y
        out = np.zeros((R, C, len(self.units) + 1, 2 + 2 * self.nb * 4), np.int32)
        for r in range(R):
            for c in range(C):
                z, x, y, k = r // 2, r % 2, c // 2, c % 2
                out[r, c, -1, 0] = x != k
                for u, unit in enumerate(self.units):
                    if z not in self.origin[unit]:
                        continue
                    there = self.origin[unit][z]
                    out[r, c, u, 0] = 1
                    out[r, c, u, 1] = (there % Y - y) % Y
                    for e in range(2):
                        rho = k ^ e
                        base = 2 * (there - z) + k - rho
                        phase = (2 * y + x - 2 * z - rho + self.half) % C
                        first = -((self.half + base) // R)
                        for n in range(self.nb):
                            w = first + n
                            b = base + R * w
                            ok = -self.half <= b < self.half
                            at = 2 + (e * self.nb + n) * 4
                            out[r, c, u, at:at + 4] = (
                                ((b + self.half) // C if ok else 0),
                                w % M,
                                (phase - b) // C,
                                ok,
                            )
        return out


def right_side(plan, terms, m, block_at):
    S, M = plan.S, plan.M
    parts = []
    for n, (_, row_shift, slot_shift, ok) in enumerate(terms):
        row = lax.rem(m + row_shift, M)
        cols = []
        for s in range(S):
            slot = s + slot_shift
            inside = jnp.logical_and(ok == 1, jnp.logical_and(slot >= 0, slot < S))
            block = block_at(n, row, jnp.clip(slot, 0, S - 1))
            cols.append(jnp.where(inside, block, jnp.zeros_like(block)))
        parts.append(jnp.concatenate(cols, axis=1))
    return jnp.concatenate(parts, axis=0)


def terms_of(plan, tab, unit, e):
    at = 2 + e * plan.nb * 4
    return [tuple(tab[unit, at + 4 * n + i] for i in range(4)) for n in range(plan.nb)]


def contract_body(plan, wanted, kinds, spans, tab, *refs):
    low, high = (0 if H in kinds else 1), (3 if D in kinds else 2)
    data, refs = refs[:len(spans)], refs[len(spans):]
    total_refs, (held, rows, sem, row_sem) = refs[:2], refs[2:]
    S, M, Y = plan.S, plan.M, plan.Y
    B = held.shape[-1]
    swapped = tab[len(plan.units), 0]
    valid = [tab[unit, 0] == 1 for unit in wanted]
    some = functools.reduce(jnp.logical_or, valid)

    def copies(use, into, into_sem):
        for i, (what, a, b) in enumerate(spans):
            a, b, first = max(a, low), min(b, high), a
            if what == use and a < b:
                yield pltpu.make_async_copy(
                    data[i].at[pl.ds(a - first, b - a)], into.at[pl.ds(a - low, b - a)], into_sem.at[a - low]
                )

    def unit_copies(u):
        return copies(("unit", u), held.at[u], sem.at[u])

    for flip in range(2):
        @pl.when(jnp.logical_and(some, swapped == flip))
        def _(flip=flip):
            for side, dy in itertools.product(range(2), range(Y)):
                into = (side ^ flip, dy)
                for copy in copies(("rows", side, dy), rows.at[into], row_sem.at[into]):
                    copy.start()
    for u in range(len(wanted)):
        @pl.when(valid[u])
        def _(u=u):
            for copy in unit_copies(u):
                copy.start()

    for total_ref in total_refs:
        total_ref[...] = jnp.zeros_like(total_ref)

    for flip in range(2):
        @pl.when(jnp.logical_and(some, swapped == flip))
        def _(flip=flip):
            for side, dy in itertools.product(range(2), range(Y)):
                into = (side ^ flip, dy)
                for copy in copies(("rows", side, dy), rows.at[into], row_sem.at[into]):
                    copy.wait()

    for u, unit in enumerate(wanted):
        @pl.when(valid[u])
        def _(u=u, unit=unit):
            for copy in unit_copies(u):
                copy.wait()
            dy = tab[unit, 1]
            for e in range(2):
                terms = terms_of(plan, tab, unit, e)

                @pl.loop(0, M, unroll=True)
                def _(m, e=e, terms=terms):
                    def left(mat):
                        return jnp.concatenate([rows[e, dy, mat - low, m, slot] for slot, _, _, _ in terms], axis=1)

                    def right(mat):
                        return right_side(plan, terms, m, lambda n, row, slot: held[u, mat - low, row, slot])

                    dot = functools.partial(jnp.dot, preferred_element_type=jnp.float32)
                    both = dot(jnp.concatenate([left(kind) for kind in kinds], axis=0), right(Q))
                    mine = left(Q)
                    for i, kind in enumerate(kinds):
                        there, back = both[i * B:(i + 1) * B], dot(mine, right(kind))
                        sums = there - back if kind == H else there + back
                        for s in range(S):
                            total_refs[e][i, m, s] += sums[:, s * B:(s + 1) * B]


def contract(plan, tab, near, far, wanted, kinds, got):
    M, S, Y = plan.M, plan.S, plan.Y
    operands, spans = [], []
    for u, unit in enumerate(wanted):
        for array, first in got[unit]:
            operands.append(array)
            spans.append((("unit", u), first, first + array.shape[0]))
    for side, lists in enumerate((near, far)):
        for dy, pieces in enumerate(lists):
            for array, first in pieces:
                operands.append(array)
                spans.append((("rows", side, dy), first, first + array.shape[0]))
    B, kind_of = operands[0].shape[-1], operands[0].dtype
    mats = 1 + len(kinds)
    specs = [pl.BlockSpec(memory_space=pl.ANY)] * len(operands)
    whole = pl.BlockSpec(memory_space=pltpu.VMEM)
    terms = 2 * M * min(len(wanted), plan.Z) * plan.nb * S * 2 * len(kinds)
    return pl.pallas_call(
        functools.partial(
            contract_body, plan, tuple(plan.units.index(unit) for unit in wanted), kinds, tuple(spans)
        ),
        in_specs=[pl.BlockSpec(memory_space=pltpu.SMEM)] + specs,
        out_specs=[whole] * 2,
        scratch_shapes=[
            pltpu.VMEM((len(wanted), mats, M, S, B, B), kind_of),
            pltpu.VMEM((2, Y, mats, M, S, B, B), kind_of),
            pltpu.SemaphoreType.DMA((len(wanted), mats)),
            pltpu.SemaphoreType.DMA((2, Y, mats)),
        ],
        out_shape=[jax.ShapeDtypeStruct((len(kinds), M, S, B, B), jnp.float32)] * 2,
        compiler_params=pltpu.CompilerParams(vmem_limit_bytes=30 * 2**20),
        cost_estimate=pl.CostEstimate(
            flops=6 * B**3 * terms,
            bytes_accessed=len(spans) * M * S * B * B * 2,
            transcendentals=0,
        ),
    )(tab, *operands)


def find(pieces, mat):
    for ref, first in pieces:
        if first <= mat < first + ref.shape[0]:
            return ref, mat - first


def last_body(plan, products, firsts, tab, kept, given, *refs):
    data, (kept_out, given_out, rows, held, sem) = refs[:-5], refs[-5:]
    S, M, Y, nb = plan.S, plan.M, plan.Y, plan.nb
    B = held.shape[-1]
    unit = len(plan.units) - 1
    valid = tab[unit, 0] == 1
    swapped = tab[unit + 1, 0]
    terms = [terms_of(plan, tab, unit, e) for e in range(2)]
    totals = kept_out, given_out
    places = {}
    for at, (name, first) in enumerate(firsts):
        places.setdefault(name, []).append((data[at], first))

    def base_copies():
        for i, ref in enumerate((kept, given)):
            source = ref.at[1 if products[0][2] == D else 0] if len(ref.shape) == 5 else ref
            yield pltpu.make_async_copy(source, totals[i], sem.at[0, i, 0])

    def unit_copies():
        for i, (_, mat, _) in enumerate(products):
            ref, index = find(places["unit"], mat)
            yield pltpu.make_async_copy(ref.at[index], held.at[i], sem.at[0, i, 1])

    def row_copies(e, pieces):
        for i, (mat, _, _) in enumerate(products):
            ref, index = find(pieces, mat)
            for n in range(nb):
                yield pltpu.make_async_copy(ref.at[index, :, terms[e][n][0]], rows.at[e, i, n], sem.at[1 + e, i, n])

    def fetch(verb):
        @pl.when(valid)
        def _():
            for copy in unit_copies():
                verb(copy)

        for flip, dy in itertools.product(range(2), range(Y)):
            @pl.when(jnp.logical_and(valid, jnp.logical_and(swapped == flip, tab[unit, 1] == dy)))
            def _(flip=flip, dy=dy):
                for side in range(2):
                    for copy in row_copies(side ^ flip, places["rows", side, dy]):
                        verb(copy)

        for copy in base_copies():
            verb(copy)

    fetch(lambda copy: copy.start())
    fetch(lambda copy: copy.wait())

    @pl.when(valid)
    def _():
        for e in (1, 0):
            @pl.loop(0, M, unroll=True)
            def _(m, e=e):
                more = 0
                for i, (_, _, kind) in enumerate(products):
                    left = jnp.concatenate([rows[e, i, n, m] for n in range(nb)], axis=1)
                    right = right_side(plan, terms[e], m, lambda n, row, slot: held[i, row, slot])
                    part = jnp.dot(left, right, preferred_element_type=jnp.float32)
                    more = more - part if kind == -1 else more + part
                for s in range(S):
                    totals[e][m, s] += more[:, s * B:(s + 1) * B]


def last(plan, tab, products, kept, given, near, far, unit):
    M, S, Y, nb = plan.M, plan.S, plan.Y, plan.nb
    lists = [("unit", unit)]
    lists += [(("rows", side, dy), pieces) for side, sides in enumerate((near, far)) for dy, pieces in enumerate(sides)]
    firsts = tuple((name, first) for name, pieces in lists for _, first in pieces)
    operands = [array for _, pieces in lists for array, _ in pieces]
    B = kept.shape[-1]
    return pl.pallas_call(
        functools.partial(last_body, plan, products, firsts),
        in_specs=[pl.BlockSpec(memory_space=pltpu.SMEM)] + [pl.BlockSpec(memory_space=pl.ANY)] * (2 + len(operands)),
        out_specs=[pl.BlockSpec(memory_space=pltpu.VMEM)] * 2,
        scratch_shapes=[
            pltpu.VMEM((2, len(products), nb, M, B, B), operands[0].dtype),
            pltpu.VMEM((len(products), M, S, B, B), operands[0].dtype),
            pltpu.SemaphoreType.DMA((3, 2, max(nb, 2))),
        ],
        out_shape=[jax.ShapeDtypeStruct((M, S, B, B), jnp.float32)] * 2,
        compiler_params=pltpu.CompilerParams(vmem_limit_bytes=30 * 2**20),
        cost_estimate=pl.CostEstimate(flops=2 * 10**10, bytes_accessed=8 * 2**20, transcendentals=0),
    )(tab, kept, given, *operands)


def keep_body(*refs):
    count = len(refs) // 2
    masks, values, out = refs[:count], refs[count:-1], refs[-1]
    m = pl.program_id(0)
    for i, value in enumerate(values):
        for s in range(value.shape[2]):
            block = value[0, 0, s]
            out[i, 0, s] = jnp.where(masks[i][m, 0, s] != 0, block, jnp.zeros_like(block))


def keep(values, masks):
    M, _, S, B, _ = values[0].shape
    return pl.pallas_call(
        keep_body,
        grid=(M,),
        in_specs=[pl.BlockSpec(memory_space=pltpu.SMEM)] * len(masks)
        + [pl.BlockSpec((1, 1, S, B, B), lambda m: (m, 0, 0, 0, 0))] * len(values),
        out_specs=pl.BlockSpec((len(values), 1, S, B, B), lambda m: (0, m, 0, 0, 0)),
        out_shape=jax.ShapeDtypeStruct((len(values), M, S, B, B), values[0].dtype),
    )(*masks, *values)


def tick_body(token, out):
    out[...] = token[...]


def tick(token, *done, cost=2 * 10**10):
    token = lax.optimization_barrier((token, *done))[0]
    return pl.pallas_call(
        tick_body,
        out_shape=jax.ShapeDtypeStruct(token.shape, token.dtype),
        cost_estimate=pl.CostEstimate(flops=cost, bytes_accessed=0, transcendentals=0),
    )(token)


def move(value, pairs):
    return lax.ppermute(value, AXES, pairs)


def after(value, *others):
    return lax.optimization_barrier((value, *others))[0]


def per_device(plan, h_blocks, p_blocks, p1_blocks, h_mask, p_mask, p1_mask):
    row, col = lax.axis_index("row"), lax.axis_index("col")
    tab = jnp.asarray(plan.table())[row, col]
    mine = keep((h_blocks, p1_blocks, p_blocks), (h_mask, p1_mask, p_mask))
    pattern = p1_mask[:, 0][:, :, None, None].astype(jnp.bfloat16)

    cross = plan.pairs(lambda z, x, y, k: (z, k, y, x))
    sibling = plan.pairs(lambda z, x, y, k: (z, x, y, 1 - k))
    x_swap = plan.pairs(lambda z, x, y, k: (z, 1 - x, y, k))
    x_pairs = plan.pairs(lambda z, x, y, k: (z, 1 - x, y, k) if x == k else (z, x, y, 1 - k))
    y_pairs = [plan.pairs(lambda z, x, y, k: (z, x, (y - dy) % plan.Y, k)) for dy in range(1, plan.Y)]

    unit = move(mine, cross)
    hops = {name: (source, plan.along_z(ends)) for name, source, ends in plan.hops}
    if not plan.quad:
        got = {"own": unit}
        for name, (source, pairs) in hops.items():
            got[name] = move(got[source], pairs)
        across = move(unit, x_pairs)
        near = [[(mine, 0)]] + [[(move(mine, pairs), 0)] for pairs in y_pairs]
        far = [[(across, 0)]] + [[(move(across, pairs), 0)] for pairs in y_pairs]
        got = {name: [(value, 0)] for name, value in got.items()}
        kept, given = contract(plan, tab, near, far, plan.units, (H, D), got)
        results = move((kept + move(given, sibling)).astype(jnp.bfloat16), cross)
        return tuple((result * pattern)[:, None] for result in results)

    token = jnp.zeros((8, 128), jnp.float32)
    flight = [unit]
    got = {"own": {Q: unit[1:], H: unit[:1]}}

    def along(names, part):
        for name in names:
            source, pairs = hops[name]
            got.setdefault(name, {})[part] = sent(got[source][part], pairs)

    def sent(value, pairs):
        result = move(after(value, token), pairs)
        group.append(result)
        return result

    def closed():
        return tick(token, *flight), group, []

    group = []
    along(("mid", "out1", "in"), Q)
    token, flight, group = closed()
    along(("mid", "out1", "in"), H)
    beside = [sent(mine, pairs) for pairs in y_pairs]
    across = sent(unit, x_pairs)
    token, flight, group = closed()
    along(("mid2", "out2"), Q)
    token, flight, group = closed()
    along(("mid2", "out2"), H)
    far_qd = [sent(across[1:], pairs) for pairs in y_pairs]
    far_h = [sent(value[:1], x_swap) for value in beside]
    token, flight, group = closed()
    along(("out3",), Q)
    token, flight, group = closed()
    along(("out3",), H)

    near = [[(mine, H)]] + [[(value, H)] for value in beside]
    far = [[(across, H)]] + [[(a, H), (b, Q)] for a, b in zip(far_h, far_qd)]
    early = ["own", "in", "mid", "out1", "mid2", "out2"]
    pieces = {name: [(parts[H], H), (parts[Q], Q)] for name, parts in got.items()}
    kept, given = contract(plan, after(tab, token), near, far, early, (H, D), pieces)
    barrier = lax.optimization_barrier
    out_qd, out_h = pieces["out3"][1:], pieces["out3"][:1]
    own, lent = last(plan, tab, ((D, Q, D), (Q, D, D)), kept, given, near, far, out_qd)
    lent = move(lent, sibling)
    own, kept = barrier((own, kept))
    kept, given = last(plan, tab, ((H, Q, H),), kept, given, near, far, out_qd)
    lent, kept = barrier((lent, kept))
    response, given = barrier(((own + lent).astype(jnp.bfloat16), given))
    response = move(response, cross)
    own, lent = last(plan, tab, ((Q, H, -1),), kept, given, near, far, out_h)
    commutator = move((own + move(lent, sibling)).astype(jnp.bfloat16), cross)
    return (commutator * pattern)[:, None], (response * pattern)[:, None]


def solution(mesh):
    blocks = P(None, "row", "col", None, None)
    masks = P(None, "row", "col")

    def run(h_blocks, p_blocks, p1_blocks, h_mask, p_mask, p1_mask):
        plan = Plan(
            mesh.shape["row"], mesh.shape["col"], h_blocks.shape[0], h_blocks.shape[2] // mesh.shape["col"]
        )
        return jax.shard_map(
            functools.partial(per_device, plan),
            mesh=mesh,
            in_specs=(blocks,) * 3 + (masks,) * 3,
            out_specs=(blocks,) * 2,
            check_vma=False,
        )(h_blocks, p_blocks, p1_blocks, h_mask, p_mask, p1_mask)

    return run
```

```python
import functools
import itertools

import jax
import jax.numpy as jnp
import numpy as np
from jax import lax
from jax.experimental import pallas as pl
from jax.experimental.pallas import tpu as pltpu
from jax.sharding import PartitionSpec as P

H, Q, D = 0, 1, 2
AXES = ("row", "col")


class Plan:
    def __init__(self, row_count, col_count, rows_dev, slot_count):
        self.R, self.C, self.M, self.S = row_count, col_count, rows_dev, slot_count
        self.Z, self.Y = row_count // 2, col_count // 2
        self.K = slot_count * col_count
        self.half = self.K // 2
        self.nb = -(-self.K // self.R)
        reach = (self.half + 1) // 2
        Z = self.Z
        ring = 2 * reach + 1 <= Z
        self.quad = Z == 4 and not ring
        if self.quad:
            inward, middle, outward = [(0, 1), (3, 2)], [(1, 2), (2, 1)], [(1, 0), (2, 3)]
            self.hops = [
                ("mid", "own", middle), ("out1", "own", outward), ("in", "own", inward),
                ("mid2", "in", middle), ("out2", "mid", outward), ("out3", "mid2", outward),
            ]
        else:
            self.hops = []
            for step in range(1, (reach if ring else Z - 1) + 1):
                for name, way in (("up", 1), ("down", -1)):
                    ends = [(z, z + way) for z in range(Z)]
                    ends = [(z, to % Z) for z, to in ends if ring or 0 <= to < Z and 0 <= z - way * (step - 1) < Z]
                    self.hops.append((name + str(step), name + str(step - 1) if step > 1 else "own", ends))
        self.origin = {"own": {z: z for z in range(Z)}}
        for name, source, ends in self.hops:
            self.origin[name] = {to: self.origin[source][z] for z, to in ends}
        self.units = list(self.origin)

    def pairs(self, target, planes=None):
        found = []
        for z in range(self.Z) if planes is None else planes:
            for x in range(2):
                for y in range(self.Y):
                    for k in range(2):
                        to = target(z, x, y, k)
                        if to is not None:
                            tz, tx, ty, tk = to
                            found.append(
                                ((2 * z + x) * self.C + 2 * y + k, (2 * tz + tx) * self.C + 2 * ty + tk)
                            )
        return found

    def along_z(self, ends):
        ends = dict(ends)
        return self.pairs(lambda z, x, y, k: (ends[z], x, y, k) if z in ends else None)

    def table(self):
        R, C, M, Y = self.R, self.C, self.M, self.Y
        out = np.zeros((R, C, len(self.units) + 1, 2 + 2 * self.nb * 4), np.int32)
        for r in range(R):
            for c in range(C):
                z, x, y, k = r // 2, r % 2, c // 2, c % 2
                out[r, c, -1, 0] = x != k
                for u, unit in enumerate(self.units):
                    if z not in self.origin[unit]:
                        continue
                    there = self.origin[unit][z]
                    out[r, c, u, 0] = 1
                    out[r, c, u, 1] = (there % Y - y) % Y
                    for e in range(2):
                        rho = k ^ e
                        base = 2 * (there - z) + k - rho
                        phase = (2 * y + x - 2 * z - rho + self.half) % C
                        first = -((self.half + base) // R)
                        for n in range(self.nb):
                            w = first + n
                            b = base + R * w
                            ok = -self.half <= b < self.half
                            at = 2 + (e * self.nb + n) * 4
                            out[r, c, u, at:at + 4] = (
                                ((b + self.half) // C if ok else 0),
                                w % M,
                                (phase - b) // C,
                                ok,
                            )
        return out


def right_side(plan, terms, m, block_at):
    S, M = plan.S, plan.M
    parts = []
    for n, (_, row_shift, slot_shift, ok) in enumerate(terms):
        row = lax.rem(m + row_shift, M)
        cols = []
        for s in range(S):
            slot = s + slot_shift
            inside = jnp.logical_and(ok == 1, jnp.logical_and(slot >= 0, slot < S))
            block = block_at(n, row, jnp.clip(slot, 0, S - 1))
            cols.append(jnp.where(inside, block, jnp.zeros_like(block)))
        parts.append(jnp.concatenate(cols, axis=1))
    return jnp.concatenate(parts, axis=0)


def terms_of(plan, tab, unit, e):
    at = 2 + e * plan.nb * 4
    return [tuple(tab[unit, at + 4 * n + i] for i in range(4)) for n in range(plan.nb)]


def contract_body(plan, wanted, kinds, spans, tab, *refs):
    low, high = (0 if H in kinds else 1), (3 if D in kinds else 2)
    data, refs = refs[:len(spans)], refs[len(spans):]
    total_refs, (held, rows, sem, row_sem) = refs[:2], refs[2:]
    S, M, Y = plan.S, plan.M, plan.Y
    B = held.shape[-1]
    swapped = tab[len(plan.units), 0]
    valid = [tab[unit, 0] == 1 for unit in wanted]
    some = functools.reduce(jnp.logical_or, valid)

    def copies(use, into, into_sem):
        for i, (what, a, b) in enumerate(spans):
            a, b, first = max(a, low), min(b, high), a
            if what == use and a < b:
                yield pltpu.make_async_copy(
                    data[i].at[pl.ds(a - first, b - a)], into.at[pl.ds(a - low, b - a)], into_sem.at[a - low]
                )

    def unit_copies(u):
        return copies(("unit", u), held.at[u], sem.at[u])

    for flip in range(2):
        @pl.when(jnp.logical_and(some, swapped == flip))
        def _(flip=flip):
            for side, dy in itertools.product(range(2), range(Y)):
                into = (side ^ flip, dy)
                for copy in copies(("rows", side, dy), rows.at[into], row_sem.at[into]):
                    copy.start()
    for u in range(len(wanted)):
        @pl.when(valid[u])
        def _(u=u):
            for copy in unit_copies(u):
                copy.start()

    for total_ref in total_refs:
        total_ref[...] = jnp.zeros_like(total_ref)

    for flip in range(2):
        @pl.when(jnp.logical_and(some, swapped == flip))
        def _(flip=flip):
            for side, dy in itertools.product(range(2), range(Y)):
                into = (side ^ flip, dy)
                for copy in copies(("rows", side, dy), rows.at[into], row_sem.at[into]):
                    copy.wait()

    for u, unit in enumerate(wanted):
        @pl.when(valid[u])
        def _(u=u, unit=unit):
            for copy in unit_copies(u):
                copy.wait()
            dy = tab[unit, 1]
            for e in range(2):
                terms = terms_of(plan, tab, unit, e)

                @pl.loop(0, M, unroll=True)
                def _(m, e=e, terms=terms):
                    def left(mat):
                        return jnp.concatenate([rows[e, dy, mat - low, m, slot] for slot, _, _, _ in terms], axis=1)

                    def right(mat):
                        return right_side(plan, terms, m, lambda n, row, slot: held[u, mat - low, row, slot])

                    dot = functools.partial(jnp.dot, preferred_element_type=jnp.float32)
                    both = dot(jnp.concatenate([left(kind) for kind in kinds], axis=0), right(Q))
                    mine = left(Q)
                    for i, kind in enumerate(kinds):
                        there, back = both[i * B:(i + 1) * B], dot(mine, right(kind))
                        sums = there - back if kind == H else there + back
                        for s in range(S):
                            total_refs[e][i, m, s] += sums[:, s * B:(s + 1) * B]


def contract(plan, tab, near, far, wanted, kinds, got):
    M, S, Y = plan.M, plan.S, plan.Y
    operands, spans = [], []
    for u, unit in enumerate(wanted):
        for array, first in got[unit]:
            operands.append(array)
            spans.append((("unit", u), first, first + array.shape[0]))
    for side, lists in enumerate((near, far)):
        for dy, pieces in enumerate(lists):
            for array, first in pieces:
                operands.append(array)
                spans.append((("rows", side, dy), first, first + array.shape[0]))
    B, kind_of = operands[0].shape[-1], operands[0].dtype
    mats = 1 + len(kinds)
    specs = [pl.BlockSpec(memory_space=pl.ANY)] * len(operands)
    whole = pl.BlockSpec(memory_space=pltpu.VMEM)
    terms = 2 * M * min(len(wanted), plan.Z) * plan.nb * S * 2 * len(kinds)
    return pl.pallas_call(
        functools.partial(
            contract_body, plan, tuple(plan.units.index(unit) for unit in wanted), kinds, tuple(spans)
        ),
        in_specs=[pl.BlockSpec(memory_space=pltpu.SMEM)] + specs,
        out_specs=[whole] * 2,
        scratch_shapes=[
            pltpu.VMEM((len(wanted), mats, M, S, B, B), kind_of),
            pltpu.VMEM((2, Y, mats, M, S, B, B), kind_of),
            pltpu.SemaphoreType.DMA((len(wanted), mats)),
            pltpu.SemaphoreType.DMA((2, Y, mats)),
        ],
        out_shape=[jax.ShapeDtypeStruct((len(kinds), M, S, B, B), jnp.float32)] * 2,
        compiler_params=pltpu.CompilerParams(vmem_limit_bytes=30 * 2**20),
        cost_estimate=pl.CostEstimate(
            flops=6 * B**3 * terms,
            bytes_accessed=len(spans) * M * S * B * B * 2,
            transcendentals=0,
        ),
    )(tab, *operands)


def find(pieces, mat):
    for ref, first in pieces:
        if first <= mat < first + ref.shape[0]:
            return ref, mat - first


def last_body(plan, products, firsts, tab, kept, given, *refs):
    data, (kept_out, given_out, rows, held, sem) = refs[:-5], refs[-5:]
    S, M, Y, nb = plan.S, plan.M, plan.Y, plan.nb
    B = held.shape[-1]
    unit = len(plan.units) - 1
    valid = tab[unit, 0] == 1
    swapped = tab[unit + 1, 0]
    terms = [terms_of(plan, tab, unit, e) for e in range(2)]
    totals = kept_out, given_out
    places = {}
    for at, (name, first) in enumerate(firsts):
        places.setdefault(name, []).append((data[at], first))

    def base_copies():
        for i, ref in enumerate((kept, given)):
            source = ref.at[1 if products[0][2] == D else 0] if len(ref.shape) == 5 else ref
            yield pltpu.make_async_copy(source, totals[i], sem.at[0, i, 0])

    def unit_copies():
        for i, (_, mat, _) in enumerate(products):
            ref, index = find(places["unit"], mat)
            yield pltpu.make_async_copy(ref.at[index], held.at[i], sem.at[0, i, 1])

    def row_copies(e, pieces):
        for i, (mat, _, _) in enumerate(products):
            ref, index = find(pieces, mat)
            for n in range(nb):
                yield pltpu.make_async_copy(ref.at[index, :, terms[e][n][0]], rows.at[e, i, n], sem.at[1 + e, i, n])

    def fetch(verb):
        @pl.when(valid)
        def _():
            for copy in unit_copies():
                verb(copy)

        for flip, dy in itertools.product(range(2), range(Y)):
            @pl.when(jnp.logical_and(valid, jnp.logical_and(swapped == flip, tab[unit, 1] == dy)))
            def _(flip=flip, dy=dy):
                for side in range(2):
                    for copy in row_copies(side ^ flip, places["rows", side, dy]):
                        verb(copy)

        for copy in base_copies():
            verb(copy)

    fetch(lambda copy: copy.start())
    fetch(lambda copy: copy.wait())

    @pl.when(valid)
    def _():
        for e in (1, 0):
            @pl.loop(0, M, unroll=True)
            def _(m, e=e):
                more = 0
                for i, (_, _, kind) in enumerate(products):
                    left = jnp.concatenate([rows[e, i, n, m] for n in range(nb)], axis=1)
                    right = right_side(plan, terms[e], m, lambda n, row, slot: held[i, row, slot])
                    part = jnp.dot(left, right, preferred_element_type=jnp.float32)
                    more = more - part if kind == -1 else more + part
                for s in range(S):
                    totals[e][m, s] += more[:, s * B:(s + 1) * B]


def last(plan, tab, products, kept, given, near, far, unit):
    M, S, Y, nb = plan.M, plan.S, plan.Y, plan.nb
    lists = [("unit", unit)]
    lists += [(("rows", side, dy), pieces) for side, sides in enumerate((near, far)) for dy, pieces in enumerate(sides)]
    firsts = tuple((name, first) for name, pieces in lists for _, first in pieces)
    operands = [array for _, pieces in lists for array, _ in pieces]
    B = kept.shape[-1]
    return pl.pallas_call(
        functools.partial(last_body, plan, products, firsts),
        in_specs=[pl.BlockSpec(memory_space=pltpu.SMEM)] + [pl.BlockSpec(memory_space=pl.ANY)] * (2 + len(operands)),
        out_specs=[pl.BlockSpec(memory_space=pltpu.VMEM)] * 2,
        scratch_shapes=[
            pltpu.VMEM((2, len(products), nb, M, B, B), operands[0].dtype),
            pltpu.VMEM((len(products), M, S, B, B), operands[0].dtype),
            pltpu.SemaphoreType.DMA((3, 2, max(nb, 2))),
        ],
        out_shape=[jax.ShapeDtypeStruct((M, S, B, B), jnp.float32)] * 2,
        compiler_params=pltpu.CompilerParams(vmem_limit_bytes=30 * 2**20),
        cost_estimate=pl.CostEstimate(flops=2 * 10**10, bytes_accessed=8 * 2**20, transcendentals=0),
    )(tab, kept, given, *operands)


def keep_body(*refs):
    count = len(refs) // 2
    masks, values, out = refs[:count], refs[count:-1], refs[-1]
    m = pl.program_id(0)
    for i, value in enumerate(values):
        for s in range(value.shape[2]):
            block = value[0, 0, s]
            out[i, 0, s] = jnp.where(masks[i][m, 0, s] != 0, block, jnp.zeros_like(block))


def keep(values, masks):
    M, _, S, B, _ = values[0].shape
    return pl.pallas_call(
        keep_body,
        grid=(M,),
        in_specs=[pl.BlockSpec(memory_space=pltpu.SMEM)] * len(masks)
        + [pl.BlockSpec((1, 1, S, B, B), lambda m: (m, 0, 0, 0, 0))] * len(values),
        out_specs=pl.BlockSpec((len(values), 1, S, B, B), lambda m: (0, m, 0, 0, 0)),
        out_shape=jax.ShapeDtypeStruct((len(values), M, S, B, B), values[0].dtype),
    )(*masks, *values)


def tick_body(token, out):
    out[...] = token[...]


def tick(token, *done, cost=2 * 10**10):
    token = lax.optimization_barrier((token, *done))[0]
    return pl.pallas_call(
        tick_body,
        out_shape=jax.ShapeDtypeStruct(token.shape, token.dtype),
        cost_estimate=pl.CostEstimate(flops=cost, bytes_accessed=0, transcendentals=0),
    )(token)


def move(value, pairs):
    return lax.ppermute(value, AXES, pairs)


def after(value, *others):
    return lax.optimization_barrier((value, *others))[0]


def per_device(plan, h_blocks, p_blocks, p1_blocks, h_mask, p_mask, p1_mask):
    row, col = lax.axis_index("row"), lax.axis_index("col")
    tab = jnp.asarray(plan.table())[row, col]
    mine = keep((h_blocks, p1_blocks, p_blocks), (h_mask, p1_mask, p_mask))
    pattern = p1_mask[:, 0][:, :, None, None].astype(jnp.bfloat16)

    cross = plan.pairs(lambda z, x, y, k: (z, k, y, x))
    sibling = plan.pairs(lambda z, x, y, k: (z, x, y, 1 - k))
    x_swap = plan.pairs(lambda z, x, y, k: (z, 1 - x, y, k))
    x_pairs = plan.pairs(lambda z, x, y, k: (z, 1 - x, y, k) if x == k else (z, x, y, 1 - k))
    y_pairs = [plan.pairs(lambda z, x, y, k: (z, x, (y - dy) % plan.Y, k)) for dy in range(1, plan.Y)]

    unit = move(mine, cross)
    hops = {name: (source, plan.along_z(ends)) for name, source, ends in plan.hops}
    if not plan.quad:
        got = {"own": unit}
        for name, (source, pairs) in hops.items():
            got[name] = move(got[source], pairs)
        across = move(unit, x_pairs)
        near = [[(mine, 0)]] + [[(move(mine, pairs), 0)] for pairs in y_pairs]
        far = [[(across, 0)]] + [[(move(across, pairs), 0)] for pairs in y_pairs]
        got = {name: [(value, 0)] for name, value in got.items()}
        kept, given = contract(plan, tab, near, far, plan.units, (H, D), got)
        results = move((kept + move(given, sibling)).astype(jnp.bfloat16), cross)
        return tuple((result * pattern)[:, None] for result in results)

    token = jnp.zeros((8, 128), jnp.float32)
    flight = [unit]
    got = {"own": {Q: unit[1:], H: unit[:1]}}

    def along(names, part):
        for name in names:
            source, pairs = hops[name]
            got.setdefault(name, {})[part] = sent(got[source][part], pairs)

    def sent(value, pairs):
        result = move(after(value, token), pairs)
        group.append(result)
        return result

    def closed():
        return tick(token, *flight), group, []

    group = []
    along(("mid", "out1", "in"), Q)
    token, flight, group = closed()
    along(("mid", "out1", "in"), H)
    beside = [sent(mine, pairs) for pairs in y_pairs]
    token, flight, group = closed()
    along(("mid2", "out2"), Q)
    across = sent(unit, x_pairs)
    token, flight, group = closed()
    along(("mid2", "out2"), H)
    far_qd = [sent(across[1:], pairs) for pairs in y_pairs]
    far_h = [sent(value[:1], x_swap) for value in beside]
    token, flight, group = closed()
    along(("out3",), Q)
    along(("out3",), H)
    token, flight, group = closed()

    near = [[(mine, H)]] + [[(value, H)] for value in beside]
    far = [[(across, H)]] + [[(a, H), (b, Q)] for a, b in zip(far_h, far_qd)]
    early = ["own", "in", "mid", "out1", "mid2", "out2"]
    pieces = {name: [(parts[H], H), (parts[Q], Q)] for name, parts in got.items()}
    kept, given = contract(plan, after(tab, token), near, far, early, (H, D), pieces)
    barrier = lax.optimization_barrier
    out_qd, out_h = pieces["out3"][1:], pieces["out3"][:1]
    own, lent = last(plan, tab, ((D, Q, D), (Q, D, D)), kept, given, near, far, out_qd)
    lent = move(lent, sibling)
    own, kept = barrier((own, kept))
    kept, given = last(plan, tab, ((H, Q, H),), kept, given, near, far, out_qd)
    lent, kept = barrier((lent, kept))
    response, given = barrier(((own + lent).astype(jnp.bfloat16), given))
    response = move(response, cross)
    own, lent = last(plan, tab, ((Q, H, -1),), kept, given, near, far, out_h)
    commutator = move((own + move(lent, sibling)).astype(jnp.bfloat16), cross)
    return (commutator * pattern)[:, None], (response * pattern)[:, None]


def solution(mesh):
    blocks = P(None, "row", "col", None, None)
    masks = P(None, "row", "col")

    def run(h_blocks, p_blocks, p1_blocks, h_mask, p_mask, p1_mask):
        plan = Plan(
            mesh.shape["row"], mesh.shape["col"], h_blocks.shape[0], h_blocks.shape[2] // mesh.shape["col"]
        )
        return jax.shard_map(
            functools.partial(per_device, plan),
            mesh=mesh,
            in_specs=(blocks,) * 3 + (masks,) * 3,
            out_specs=(blocks,) * 2,
            check_vma=False,
        )(h_blocks, p_blocks, p1_blocks, h_mask, p_mask, p1_mask)

    return run
```

```python
import functools
import itertools

import jax
import jax.numpy as jnp
import numpy as np
from jax import lax
from jax.experimental import pallas as pl
from jax.experimental.pallas import tpu as pltpu
from jax.sharding import PartitionSpec as P

H, Q, D = 0, 1, 2
AXES = ("row", "col")


class Plan:
    def __init__(self, row_count, col_count, rows_dev, slot_count):
        self.R, self.C, self.M, self.S = row_count, col_count, rows_dev, slot_count
        self.Z, self.Y = row_count // 2, col_count // 2
        self.K = slot_count * col_count
        self.half = self.K // 2
        self.nb = -(-self.K // self.R)
        reach = (self.half + 1) // 2
        Z = self.Z
        ring = 2 * reach + 1 <= Z
        self.quad = Z == 4 and not ring
        if self.quad:
            inward, middle, outward = [(0, 1), (3, 2)], [(1, 2), (2, 1)], [(1, 0), (2, 3)]
            self.hops = [
                ("mid", "own", middle), ("out1", "own", outward), ("in", "own", inward),
                ("mid2", "in", middle), ("out2", "mid", outward), ("out3", "mid2", outward),
            ]
        else:
            self.hops = []
            for step in range(1, (reach if ring else Z - 1) + 1):
                for name, way in (("up", 1), ("down", -1)):
                    ends = [(z, z + way) for z in range(Z)]
                    ends = [(z, to % Z) for z, to in ends if ring or 0 <= to < Z and 0 <= z - way * (step - 1) < Z]
                    self.hops.append((name + str(step), name + str(step - 1) if step > 1 else "own", ends))
        self.origin = {"own": {z: z for z in range(Z)}}
        for name, source, ends in self.hops:
            self.origin[name] = {to: self.origin[source][z] for z, to in ends}
        self.units = list(self.origin)

    def pairs(self, target, planes=None):
        found = []
        for z in range(self.Z) if planes is None else planes:
            for x in range(2):
                for y in range(self.Y):
                    for k in range(2):
                        to = target(z, x, y, k)
                        if to is not None:
                            tz, tx, ty, tk = to
                            found.append(
                                ((2 * z + x) * self.C + 2 * y + k, (2 * tz + tx) * self.C + 2 * ty + tk)
                            )
        return found

    def along_z(self, ends):
        ends = dict(ends)
        return self.pairs(lambda z, x, y, k: (ends[z], x, y, k) if z in ends else None)

    def table(self):
        R, C, M, Y = self.R, self.C, self.M, self.Y
        out = np.zeros((R, C, len(self.units) + 1, 2 + 2 * self.nb * 4), np.int32)
        for r in range(R):
            for c in range(C):
                z, x, y, k = r // 2, r % 2, c // 2, c % 2
                out[r, c, -1, 0] = x != k
                for u, unit in enumerate(self.units):
                    if z not in self.origin[unit]:
                        continue
                    there = self.origin[unit][z]
                    out[r, c, u, 0] = 1
                    out[r, c, u, 1] = (there % Y - y) % Y
                    for e in range(2):
                        rho = k ^ e
                        base = 2 * (there - z) + k - rho
                        phase = (2 * y + x - 2 * z - rho + self.half) % C
                        first = -((self.half + base) // R)
                        for n in range(self.nb):
                            w = first + n
                            b = base + R * w
                            ok = -self.half <= b < self.half
                            at = 2 + (e * self.nb + n) * 4
                            out[r, c, u, at:at + 4] = (
                                ((b + self.half) // C if ok else 0),
                                w % M,
                                (phase - b) // C,
                                ok,
                            )
        return out


def right_side(plan, terms, m, block_at):
    S, M = plan.S, plan.M
    parts = []
    for n, (_, row_shift, slot_shift, ok) in enumerate(terms):
        row = lax.rem(m + row_shift, M)
        cols = []
        for s in range(S):
            slot = s + slot_shift
            inside = jnp.logical_and(ok == 1, jnp.logical_and(slot >= 0, slot < S))
            block = block_at(n, row, jnp.clip(slot, 0, S - 1))
            cols.append(jnp.where(inside, block, jnp.zeros_like(block)))
        parts.append(jnp.concatenate(cols, axis=1))
    return jnp.concatenate(parts, axis=0)


def terms_of(plan, tab, unit, e):
    at = 2 + e * plan.nb * 4
    return [tuple(tab[unit, at + 4 * n + i] for i in range(4)) for n in range(plan.nb)]


def contract_body(plan, wanted, kinds, spans, tab, *refs):
    low, high = (0 if H in kinds else 1), (3 if D in kinds else 2)
    data, refs = refs[:len(spans)], refs[len(spans):]
    total_refs, (held, rows, sem, row_sem) = refs[:2], refs[2:]
    S, M, Y = plan.S, plan.M, plan.Y
    B = held.shape[-1]
    swapped = tab[len(plan.units), 0]
    valid = [tab[unit, 0] == 1 for unit in wanted]
    some = functools.reduce(jnp.logical_or, valid)

    def copies(use, into, into_sem):
        for i, (what, a, b) in enumerate(spans):
            a, b, first = max(a, low), min(b, high), a
            if what == use and a < b:
                yield pltpu.make_async_copy(
                    data[i].at[pl.ds(a - first, b - a)], into.at[pl.ds(a - low, b - a)], into_sem.at[a - low]
                )

    def unit_copies(u):
        return copies(("unit", u), held.at[u], sem.at[u])

    for flip in range(2):
        @pl.when(jnp.logical_and(some, swapped == flip))
        def _(flip=flip):
            for side, dy in itertools.product(range(2), range(Y)):
                into = (side ^ flip, dy)
                for copy in copies(("rows", side, dy), rows.at[into], row_sem.at[into]):
                    copy.start()
    for u in range(len(wanted)):
        @pl.when(valid[u])
        def _(u=u):
            for copy in unit_copies(u):
                copy.start()

    for total_ref in total_refs:
        total_ref[...] = jnp.zeros_like(total_ref)

    for flip in range(2):
        @pl.when(jnp.logical_and(some, swapped == flip))
        def _(flip=flip):
            for side, dy in itertools.product(range(2), range(Y)):
                into = (side ^ flip, dy)
                for copy in copies(("rows", side, dy), rows.at[into], row_sem.at[into]):
                    copy.wait()

    for u, unit in enumerate(wanted):
        @pl.when(valid[u])
        def _(u=u, unit=unit):
            for copy in unit_copies(u):
                copy.wait()
            dy = tab[unit, 1]
            for e in range(2):
                terms = terms_of(plan, tab, unit, e)

                @pl.loop(0, M, unroll=True)
                def _(m, e=e, terms=terms):
                    def left(mat):
                        return jnp.concatenate([rows[e, dy, mat - low, m, slot] for slot, _, _, _ in terms], axis=1)

                    def right(mat):
                        return right_side(plan, terms, m, lambda n, row, slot: held[u, mat - low, row, slot])

                    dot = functools.partial(jnp.dot, preferred_element_type=jnp.float32)
                    both = dot(jnp.concatenate([left(kind) for kind in kinds], axis=0), right(Q))
                    mine = left(Q)
                    for i, kind in enumerate(kinds):
                        there, back = both[i * B:(i + 1) * B], dot(mine, right(kind))
                        sums = there - back if kind == H else there + back
                        for s in range(S):
                            total_refs[e][i, m, s] += sums[:, s * B:(s + 1) * B]


def contract(plan, tab, near, far, wanted, kinds, got):
    M, S, Y = plan.M, plan.S, plan.Y
    operands, spans = [], []
    for u, unit in enumerate(wanted):
        for array, first in got[unit]:
            operands.append(array)
            spans.append((("unit", u), first, first + array.shape[0]))
    for side, lists in enumerate((near, far)):
        for dy, pieces in enumerate(lists):
            for array, first in pieces:
                operands.append(array)
                spans.append((("rows", side, dy), first, first + array.shape[0]))
    B, kind_of = operands[0].shape[-1], operands[0].dtype
    mats = 1 + len(kinds)
    specs = [pl.BlockSpec(memory_space=pl.ANY)] * len(operands)
    whole = pl.BlockSpec(memory_space=pltpu.VMEM)
    terms = 2 * M * min(len(wanted), plan.Z) * plan.nb * S * 2 * len(kinds)
    return pl.pallas_call(
        functools.partial(
            contract_body, plan, tuple(plan.units.index(unit) for unit in wanted), kinds, tuple(spans)
        ),
        in_specs=[pl.BlockSpec(memory_space=pltpu.SMEM)] + specs,
        out_specs=[whole] * 2,
        scratch_shapes=[
            pltpu.VMEM((len(wanted), mats, M, S, B, B), kind_of),
            pltpu.VMEM((2, Y, mats, M, S, B, B), kind_of),
            pltpu.SemaphoreType.DMA((len(wanted), mats)),
            pltpu.SemaphoreType.DMA((2, Y, mats)),
        ],
        out_shape=[jax.ShapeDtypeStruct((len(kinds), M, S, B, B), jnp.float32)] * 2,
        compiler_params=pltpu.CompilerParams(vmem_limit_bytes=30 * 2**20),
        cost_estimate=pl.CostEstimate(
            flops=6 * B**3 * terms,
            bytes_accessed=len(spans) * M * S * B * B * 2,
            transcendentals=0,
        ),
    )(tab, *operands)


def find(pieces, mat):
    for ref, first in pieces:
        if first <= mat < first + ref.shape[0]:
            return ref, mat - first


def last_body(plan, products, firsts, tab, kept, given, *refs):
    data, (kept_out, given_out, rows, held, sem) = refs[:-5], refs[-5:]
    S, M, Y, nb = plan.S, plan.M, plan.Y, plan.nb
    B = held.shape[-1]
    unit = len(plan.units) - 1
    valid = tab[unit, 0] == 1
    swapped = tab[unit + 1, 0]
    terms = [terms_of(plan, tab, unit, e) for e in range(2)]
    totals = kept_out, given_out
    places = {}
    for at, (name, first) in enumerate(firsts):
        places.setdefault(name, []).append((data[at], first))

    def base_copies():
        for i, ref in enumerate((kept, given)):
            source = ref.at[1 if products[0][2] == D else 0] if len(ref.shape) == 5 else ref
            yield pltpu.make_async_copy(source, totals[i], sem.at[0, i, 0])

    def unit_copies():
        for i, (_, mat, _) in enumerate(products):
            ref, index = find(places["unit"], mat)
            yield pltpu.make_async_copy(ref.at[index], held.at[i], sem.at[0, i, 1])

    def row_copies(e, pieces):
        for i, (mat, _, _) in enumerate(products):
            ref, index = find(pieces, mat)
            for n in range(nb):
                yield pltpu.make_async_copy(ref.at[index, :, terms[e][n][0]], rows.at[e, i, n], sem.at[1 + e, i, n])

    def fetch(verb):
        @pl.when(valid)
        def _():
            for copy in unit_copies():
                verb(copy)

        for flip, dy in itertools.product(range(2), range(Y)):
            @pl.when(jnp.logical_and(valid, jnp.logical_and(swapped == flip, tab[unit, 1] == dy)))
            def _(flip=flip, dy=dy):
                for side in range(2):
                    for copy in row_copies(side ^ flip, places["rows", side, dy]):
                        verb(copy)

        for copy in base_copies():
            verb(copy)

    fetch(lambda copy: copy.start())
    fetch(lambda copy: copy.wait())

    @pl.when(valid)
    def _():
        for e in (1, 0):
            @pl.loop(0, M, unroll=True)
            def _(m, e=e):
                more = 0
                for i, (_, _, kind) in enumerate(products):
                    left = jnp.concatenate([rows[e, i, n, m] for n in range(nb)], axis=1)
                    right = right_side(plan, terms[e], m, lambda n, row, slot: held[i, row, slot])
                    part = jnp.dot(left, right, preferred_element_type=jnp.float32)
                    more = more - part if kind == -1 else more + part
                for s in range(S):
                    totals[e][m, s] += more[:, s * B:(s + 1) * B]


def last(plan, tab, products, kept, given, near, far, unit):
    M, S, Y, nb = plan.M, plan.S, plan.Y, plan.nb
    lists = [("unit", unit)]
    lists += [(("rows", side, dy), pieces) for side, sides in enumerate((near, far)) for dy, pieces in enumerate(sides)]
    firsts = tuple((name, first) for name, pieces in lists for _, first in pieces)
    operands = [array for _, pieces in lists for array, _ in pieces]
    B = kept.shape[-1]
    return pl.pallas_call(
        functools.partial(last_body, plan, products, firsts),
        in_specs=[pl.BlockSpec(memory_space=pltpu.SMEM)] + [pl.BlockSpec(memory_space=pl.ANY)] * (2 + len(operands)),
        out_specs=[pl.BlockSpec(memory_space=pltpu.VMEM)] * 2,
        scratch_shapes=[
            pltpu.VMEM((2, len(products), nb, M, B, B), operands[0].dtype),
            pltpu.VMEM((len(products), M, S, B, B), operands[0].dtype),
            pltpu.SemaphoreType.DMA((3, 2, max(nb, 2))),
        ],
        out_shape=[jax.ShapeDtypeStruct((M, S, B, B), jnp.float32)] * 2,
        compiler_params=pltpu.CompilerParams(vmem_limit_bytes=30 * 2**20),
        cost_estimate=pl.CostEstimate(flops=2 * 10**10, bytes_accessed=8 * 2**20, transcendentals=0),
    )(tab, kept, given, *operands)


def keep_body(*refs):
    count = len(refs) // 2
    masks, values, out = refs[:count], refs[count:-1], refs[-1]
    m = pl.program_id(0)
    for i, value in enumerate(values):
        for s in range(value.shape[2]):
            block = value[0, 0, s]
            out[i, 0, s] = jnp.where(masks[i][m, 0, s] != 0, block, jnp.zeros_like(block))


def keep(values, masks):
    M, _, S, B, _ = values[0].shape
    return pl.pallas_call(
        keep_body,
        grid=(M,),
        in_specs=[pl.BlockSpec(memory_space=pltpu.SMEM)] * len(masks)
        + [pl.BlockSpec((1, 1, S, B, B), lambda m: (m, 0, 0, 0, 0))] * len(values),
        out_specs=pl.BlockSpec((len(values), 1, S, B, B), lambda m: (0, m, 0, 0, 0)),
        out_shape=jax.ShapeDtypeStruct((len(values), M, S, B, B), values[0].dtype),
    )(*masks, *values)


def tick_body(token, out):
    out[...] = token[...]


def tick(token, *done, cost=2 * 10**10):
    token = lax.optimization_barrier((token, *done))[0]
    return pl.pallas_call(
        tick_body,
        out_shape=jax.ShapeDtypeStruct(token.shape, token.dtype),
        cost_estimate=pl.CostEstimate(flops=cost, bytes_accessed=0, transcendentals=0),
    )(token)


def move(value, pairs):
    return lax.ppermute(value, AXES, pairs)


def after(value, *others):
    return lax.optimization_barrier((value, *others))[0]


def per_device(plan, h_blocks, p_blocks, p1_blocks, h_mask, p_mask, p1_mask):
    row, col = lax.axis_index("row"), lax.axis_index("col")
    tab = jnp.asarray(plan.table())[row, col]
    mine = keep((h_blocks, p1_blocks, p_blocks), (h_mask, p1_mask, p_mask))
    pattern = p1_mask[:, 0][:, :, None, None].astype(jnp.bfloat16)

    cross = plan.pairs(lambda z, x, y, k: (z, k, y, x))
    sibling = plan.pairs(lambda z, x, y, k: (z, x, y, 1 - k))
    x_swap = plan.pairs(lambda z, x, y, k: (z, 1 - x, y, k))
    x_pairs = plan.pairs(lambda z, x, y, k: (z, 1 - x, y, k) if x == k else (z, x, y, 1 - k))
    y_pairs = [plan.pairs(lambda z, x, y, k: (z, x, (y - dy) % plan.Y, k)) for dy in range(1, plan.Y)]

    unit = move(mine, cross)
    hops = {name: (source, plan.along_z(ends)) for name, source, ends in plan.hops}
    if not plan.quad:
        got = {"own": unit}
        for name, (source, pairs) in hops.items():
            got[name] = move(got[source], pairs)
        across = move(unit, x_pairs)
        near = [[(mine, 0)]] + [[(move(mine, pairs), 0)] for pairs in y_pairs]
        far = [[(across, 0)]] + [[(move(across, pairs), 0)] for pairs in y_pairs]
        got = {name: [(value, 0)] for name, value in got.items()}
        kept, given = contract(plan, tab, near, far, plan.units, (H, D), got)
        results = move((kept + move(given, sibling)).astype(jnp.bfloat16), cross)
        return tuple((result * pattern)[:, None] for result in results)

    token = jnp.zeros((8, 128), jnp.float32)
    flight = [unit]
    got = {"own": {Q: unit[1:], H: unit[:1]}}

    def along(names, part):
        for name in names:
            source, pairs = hops[name]
            got.setdefault(name, {})[part] = sent(got[source][part], pairs)

    def sent(value, pairs):
        result = move(after(value, token), pairs)
        group.append(result)
        return result

    def closed():
        return tick(token, *flight), group, []

    group = []
    along(("mid", "out1", "in"), Q)
    token, flight, group = closed()
    along(("mid", "out1", "in"), H)
    beside = [sent(mine, pairs) for pairs in y_pairs]
    token, flight, group = closed()
    along(("mid2", "out2"), Q)
    across = sent(unit, x_pairs)
    token, flight, group = closed()
    along(("mid2", "out2"), H)
    far_hq = [sent(across[:2], pairs) for pairs in y_pairs]
    far_d = [sent(value[2:], x_swap) for value in beside]
    token, flight, group = closed()
    along(("out3",), Q)
    along(("out3",), H)
    token, flight, group = closed()

    near = [[(mine, H)]] + [[(value, H)] for value in beside]
    far = [[(across, H)]] + [[(a, H), (b, D)] for a, b in zip(far_hq, far_d)]
    early = ["own", "in", "mid", "out1", "mid2", "out2"]
    pieces = {name: [(parts[H], H), (parts[Q], Q)] for name, parts in got.items()}
    kept, given = contract(plan, after(tab, token), near, far, early, (H, D), pieces)
    barrier = lax.optimization_barrier
    out_qd, out_h = pieces["out3"][1:], pieces["out3"][:1]
    own, lent = last(plan, tab, ((D, Q, D), (Q, D, D)), kept, given, near, far, out_qd)
    lent = move(lent, sibling)
    own, kept = barrier((own, kept))
    kept, given = last(plan, tab, ((H, Q, H),), kept, given, near, far, out_qd)
    lent, kept = barrier((lent, kept))
    response, given = barrier(((own + lent).astype(jnp.bfloat16), given))
    response = move(response, cross)
    own, lent = last(plan, tab, ((Q, H, -1),), kept, given, near, far, out_h)
    commutator = move((own + move(lent, sibling)).astype(jnp.bfloat16), cross)
    return (commutator * pattern)[:, None], (response * pattern)[:, None]


def solution(mesh):
    blocks = P(None, "row", "col", None, None)
    masks = P(None, "row", "col")

    def run(h_blocks, p_blocks, p1_blocks, h_mask, p_mask, p1_mask):
        plan = Plan(
            mesh.shape["row"], mesh.shape["col"], h_blocks.shape[0], h_blocks.shape[2] // mesh.shape["col"]
        )
        return jax.shard_map(
            functools.partial(per_device, plan),
            mesh=mesh,
            in_specs=(blocks,) * 3 + (masks,) * 3,
            out_specs=(blocks,) * 2,
            check_vma=False,
        )(h_blocks, p_blocks, p1_blocks, h_mask, p_mask, p1_mask)

    return run
```
